32 devices in a mesh: grp: 2 (over x), row: 2 (over core), col: 8 (over z, y).
Axes of the slice: x: 2, y: 2, z: 4, core: 2. Of those that a mesh axis runs over, the one named last changes fastest.
Arguments:
- tokens: bfloat16 [256, 4096], P(('grp', 'col'), 'row'), parts along dimension 0, may hold values from -6 to 6
- cotangent: bfloat16 [256, 4096], P(('grp', 'col'), 'row'), parts along dimension 0, may hold values from -6 to 6
- adapter_index: int32 [256], P('grp'), parts along dimension 0, may hold values from 0 to 7
- retain_mask: int32 [3, 224, 64], P(None, 'col', 'row'), may hold values 0 or 1
- gate_weight: bfloat16 [14336, 4096], P('col', 'row'), may hold values from -0.09375 to 0.09375
- up_weight: bfloat16 [14336, 4096], P('col', 'row'), may hold values from -0.09375 to 0.09375
- down_weight: bfloat16 [14336, 4096], P('col', 'row'), may hold values from -0.046875 to 0.046875
- adapter_up_input: bfloat16 [4096, 256], P('row'), may hold values from -0.09375 to 0.09375
- adapter_up_output: bfloat16 [256, 14336], P(None, 'col'), may hold values from -0.125 to 0.125
- adapter_down_input: bfloat16 [14336, 256], P('col'), may hold values from -0.046875 to 0.046875
- adapter_down_output: bfloat16 [256, 4096], P(None, 'row'), may hold values from -0.25 to 0.25
Outputs:
- layer_output: bfloat16 [256, 4096], P(('grp', 'col'), 'row'), parts along dimension 0
- token_gradient: bfloat16 [256, 4096], P(('grp', 'col'), 'row'), parts along dimension 0
- grad_up_in: bfloat16 [8192, 256], P(('grp', 'row')), parts along dimension 0
- grad_up_out: bfloat16 [512, 14336], P('grp', 'col'), parts along dimension 0
- grad_down_in: bfloat16 [28672, 256], P(('grp', 'col')), parts along dimension 0
- grad_down_out: bfloat16 [512, 4096], P('grp', 'row'), parts along dimension 0
The draws below stay inside these ranges and needn't reach their ends.
There are 2 independent parts, one for each index of `grp`. The reference program is written for one: setup_inputs(seed, part) draws one part's arguments, and reference() takes and returns one part's arrays. A program takes and returns all parts, laid end to end along the dimension named above; an argument that names none is the same for every part. Nothing has to cross between parts.
All inputs are finite; a program needn't handle non-finite values. No bound on the sum of `retain_mask` on one device may be relied on, other than what follows from the above.
Results may differ from the reference program's by a relative error of at most 0.02.
Values may be sent and summed in bfloat16 or wider, within the bound.
A program may use at most 192 MiB of HBM per device.

```python
import jax
import jax.numpy as jnp
from jax import lax

MODEL_WIDTH = 4096
HIDDEN_UNITS = 14336
BLOCK = 64
REWARD_ADAPTERS = 8
ADAPTER_RANK = 32
TOKENS = 128
N_COL = 8


def set_ends(result, own_key, smallest, largest):
    longest = result.shape.index(max(result.shape))
    spots = []
    for shift in (0, 1):
        where = [jax.random.randint(jax.random.fold_in(own_key, axis), (), 0, length) for axis, length in enumerate(result.shape)]
        where[longest] = (where[longest] + shift) % result.shape[longest]
        spots.append(tuple(where))
    return result.at[spots[0]].set(smallest).at[spots[1]].set(largest)


def shard_levels(key, shape, cuts, smallest, high):
    gain = 1.0
    for position, parts in cuts:
        draws = jax.random.uniform(jax.random.fold_in(jax.random.fold_in(key, 6), position), (parts,), jnp.float32, smallest / len(cuts), high / len(cuts))
        gain = gain * jnp.repeat(jnp.exp(draws), shape[position] // parts).reshape((-1,) + (1,) * (len(shape) - 1 - position))
    return gain


def noise(rng, dims, width, bound, pieces=(), held_as=jnp.bfloat16):
    level = shard_levels(rng, dims, pieces, -0.22, 0.18) if pieces else 1.0
    drawn = jax.random.normal(rng, dims, jnp.float32) * width * level
    return jnp.minimum(jnp.maximum(drawn, -bound), bound).astype(held_as)


def setup_inputs(seed: int = 0, part: int = 0) -> dict:
    key_of = jax.random.split(jax.random.key(seed), 12)
    part_splits = jax.random.split(jax.random.fold_in(key_of[11], part), 12)
    return {
        "tokens": noise(part_splits[0], (TOKENS, MODEL_WIDTH), 1.0, 6.0, ((0, 8), (1, 2))),
        "cotangent": noise(part_splits[1], (TOKENS, MODEL_WIDTH), 1.0, 6.0, ((0, 8), (1, 2))),
        "adapter_index": set_ends(jax.random.randint(part_splits[2], (TOKENS,), 0, REWARD_ADAPTERS), jax.random.fold_in(part_splits[2], 1), 0, REWARD_ADAPTERS - 1).astype(jnp.int32),
        "retain_mask": set_ends((jax.random.randint(key_of[3], (3, HIDDEN_UNITS // BLOCK, MODEL_WIDTH // BLOCK), 0, 2) < 1).astype(jnp.int32), jax.random.fold_in(key_of[3], 1), 0, 1),
        "gate_weight": noise(key_of[4], (HIDDEN_UNITS, MODEL_WIDTH), MODEL_WIDTH ** -0.5, 0.09375, ((0, 8), (1, 2))),
        "up_weight": noise(key_of[5], (HIDDEN_UNITS, MODEL_WIDTH), MODEL_WIDTH ** -0.5, 0.09375, ((0, 8), (1, 2))),
        "down_weight": noise(key_of[6], (HIDDEN_UNITS, MODEL_WIDTH), HIDDEN_UNITS ** -0.5, 0.046875, ((0, 8), (1, 2))),
        "adapter_up_input": noise(key_of[7], (MODEL_WIDTH, REWARD_ADAPTERS * ADAPTER_RANK), MODEL_WIDTH ** -0.5, 0.09375, ((0, 2),)),
        "adapter_up_output": noise(key_of[8], (REWARD_ADAPTERS * ADAPTER_RANK, HIDDEN_UNITS), (HIDDEN_UNITS // 8) ** -0.5, 0.125, ((1, 8),)),
        "adapter_down_input": noise(key_of[9], (HIDDEN_UNITS, REWARD_ADAPTERS * ADAPTER_RANK), HIDDEN_UNITS ** -0.5, 0.046875, ((0, 8),)),
        "adapter_down_output": noise(key_of[10], (REWARD_ADAPTERS * ADAPTER_RANK, MODEL_WIDTH), (MODEL_WIDTH // 8) ** -0.5, 0.25, ((1, 2),)),
    }


def expand(retain_mask, which):
    grid = retain_mask[which].astype(jnp.bfloat16)
    return jnp.repeat(jnp.repeat(grid, BLOCK, axis=0), BLOCK, axis=1)


def rounded(value):
    narrow = lax.optimization_barrier(value.astype(jnp.bfloat16))
    return narrow.astype(jnp.float32)


def window_sum(slice_term):
    slice_width = HIDDEN_UNITS // N_COL

    def accumulate(slice_index, running):
        first_unit = jnp.asarray(slice_index).astype(jnp.int32) * slice_width
        return running + rounded(slice_term(first_unit, slice_width))

    zero_sum = jnp.zeros((TOKENS, MODEL_WIDTH), jnp.float32)
    return lax.fori_loop(0, N_COL, accumulate, zero_sum)


def reference(tokens, cotangent, adapter_index, retain_mask, gate_weight, up_weight, down_weight, adapter_up_input, adapter_up_output, adapter_down_input, adapter_down_output):
    gate_kept = gate_weight * expand(retain_mask, 0)
    up_retained = up_weight * expand(retain_mask, 1)
    down_retained = down_weight * expand(retain_mask, 2)
    columns = jnp.arange(REWARD_ADAPTERS * ADAPTER_RANK, dtype=jnp.int32) // ADAPTER_RANK
    member_choose = (adapter_index[:, None] == columns[None, :]).astype(jnp.float32)
    gate_signal = jnp.dot(tokens, gate_kept.T, preferred_element_type=jnp.float32)
    up_lowrank = (member_choose * jnp.dot(tokens, adapter_up_input, preferred_element_type=jnp.float32)).astype(jnp.bfloat16)
    up_activation = jnp.dot(tokens, up_retained.T, preferred_element_type=jnp.float32) + jnp.dot(up_lowrank, adapter_up_output, preferred_element_type=jnp.float32)
    sigmoid_gate = jax.nn.sigmoid(gate_signal)
    activated = gate_signal * sigmoid_gate
    hidden_state = (activated * up_activation).astype(jnp.bfloat16)
    down_lowrank = (member_choose * jnp.dot(hidden_state, adapter_down_input, preferred_element_type=jnp.float32)).astype(jnp.bfloat16)

    def down_window(first_unit, slice_width):
        part_hidden = lax.dynamic_slice_in_dim(hidden_state, first_unit, slice_width, 1)
        part_weight = lax.dynamic_slice_in_dim(down_retained, first_unit, slice_width, 0)
        return jnp.dot(part_hidden, part_weight, preferred_element_type=jnp.float32)

    layer_output = (window_sum(down_window) + jnp.dot(down_lowrank, adapter_down_output, preferred_element_type=jnp.float32)).astype(jnp.bfloat16)
    lowrank_reverse = (member_choose * jnp.dot(cotangent, adapter_down_output.T, preferred_element_type=jnp.float32)).astype(jnp.bfloat16)
    hidden_gradient = jnp.dot(cotangent, down_retained.T, preferred_element_type=jnp.float32) + jnp.dot(lowrank_reverse, adapter_down_input.T, preferred_element_type=jnp.float32)
    grad_gate = (hidden_gradient * up_activation * sigmoid_gate * (1.0 + gate_signal * (1.0 - sigmoid_gate))).astype(jnp.bfloat16)
    up_gradient = (hidden_gradient * activated).astype(jnp.bfloat16)
    lowrank_gradient = (member_choose * jnp.dot(up_gradient, adapter_up_output.T, preferred_element_type=jnp.float32)).astype(jnp.bfloat16)

    def input_window(first_unit, slice_width):
        part_gate = lax.dynamic_slice_in_dim(grad_gate, first_unit, slice_width, 1)
        part_up = lax.dynamic_slice_in_dim(up_gradient, first_unit, slice_width, 1)
        gate_rows = lax.dynamic_slice_in_dim(gate_kept, first_unit, slice_width, 0)
        up_rows = lax.dynamic_slice_in_dim(up_retained, first_unit, slice_width, 0)
        return jnp.dot(part_gate, gate_rows, preferred_element_type=jnp.float32) + jnp.dot(part_up, up_rows, preferred_element_type=jnp.float32)

    token_gradient = (window_sum(input_window) + jnp.dot(lowrank_gradient, adapter_up_input.T, preferred_element_type=jnp.float32)).astype(jnp.bfloat16)
    grad_up_in = jnp.dot(tokens.T, lowrank_gradient, preferred_element_type=jnp.float32).astype(jnp.bfloat16)
    grad_up_out = jnp.dot(up_lowrank.T, up_gradient, preferred_element_type=jnp.float32).astype(jnp.bfloat16)
    grad_down_in = jnp.dot(hidden_state.T, lowrank_reverse, preferred_element_type=jnp.float32).astype(jnp.bfloat16)
    grad_down_out = jnp.dot(down_lowrank.T, cotangent, preferred_element_type=jnp.float32).astype(jnp.bfloat16)
    return (layer_output, token_gradient, grad_up_in, grad_up_out, grad_down_in, grad_down_out)
```

```python
import functools

import jax
import jax.numpy as jnp
from jax import lax
from jax.experimental import pallas as pl
from jax.experimental.pallas import tpu as pltpu
from jax.sharding import PartitionSpec as P

BLOCK = 64
ADAPTER_RANK = 32
MESH = pl.DeviceIdType.MESH
BF16 = jnp.bfloat16
F32 = jnp.float32


def mm(a, b, ca, cb):
    return lax.dot_general(a, b, (((ca,), (cb,)), ((), ())), preferred_element_type=F32)


def kernel(
    n,
    tok_ref, cot_ref, index_ref, mask_ref, gate_hbm, up_hbm, down_hbm, ui_hbm, uo_hbm, di_hbm, do_hbm,
    out_ref, tg_ref, gui_ref, guo_ref, gdi_ref, gdo_ref,
    w, ui, uo, di, do, em, sel, xg, ps, pr, rs, rr, ur, rk, hs, rp, rrb, rg, ob, rb,
    w_sem, a_sem, ag_send, ag_recv, row_send, row_recv, rank_send, rank_recv, rg_send, rg_recv, rs_send, rs_recv,
):
    own = tok_ref.shape[0]
    units, width = gate_hbm.shape
    tokens = own * n
    c = lax.axis_index("col")
    r = lax.axis_index("row")
    fc = 256 if units % 256 == 0 else units
    nfc = units // fc
    dc = 512
    ndc = width // dc

    def rows_of(p):
        return pl.ds(pl.multiple_of(p * own, own), own)

    def fch(j):
        return pl.ds(pl.multiple_of(j * fc, fc), fc) if nfc > 1 else slice(None)

    def peers(body):
        def step(k, carry):
            body(lax.rem(c + k, n))
            return carry
        lax.fori_loop(1, n, step, 0)

    def loop(count, body):
        if count == 1:
            body(0)
        else:
            def step(j, carry):
                body(j)
                return carry
            lax.fori_loop(0, count, step, 0)

    mine = rows_of(c)

    def w_copy(k, j):
        return pltpu.make_async_copy((gate_hbm, up_hbm, down_hbm)[k].at[fch(j)], w.at[k, fch(j)], w_sem.at[k, j])

    a_copies = [
        pltpu.make_async_copy(src, dst, a_sem.at[i])
        for i, (src, dst) in enumerate(((ui_hbm, ui), (do_hbm, do), (uo_hbm, uo), (di_hbm, di)))
    ]
    for k in range(3):
        loop(nfc, lambda j, k=k: w_copy(k, j).start())
        if k == 0:
            for copy in a_copies:
                copy.start()

    barrier = pltpu.get_barrier_semaphore()
    peers(lambda p: pl.semaphore_signal(barrier, inc=1, device_id={"col": p}, device_id_type=MESH))
    pl.semaphore_signal(barrier, inc=1, device_id={"row": 1 - r}, device_id_type=MESH)
    xg[0, mine] = tok_ref[...]
    xg[1, mine] = cot_ref[...]
    pl.semaphore_wait(barrier, n)

    def ag(owner, p):
        part = xg.at[:, rows_of(owner)]
        return pltpu.make_async_remote_copy(part, part, ag_send.at[p], ag_recv.at[owner], device_id={"col": p}, device_id_type=MESH)

    peers(lambda p: ag(c, p).start())

    member = lax.broadcasted_iota(jnp.int32, (tokens, sel.shape[1]), 1) // ADAPTER_RANK
    sel[...] = jnp.where(index_ref[...] == member, 1.0, 0.0).astype(F32)
    blocks = mask_ref.shape[2]
    spread = (
        lax.broadcasted_iota(jnp.int32, (blocks, width), 1) // BLOCK
        == lax.broadcasted_iota(jnp.int32, (blocks, width), 0)
    ).astype(F32).astype(BF16)
    for k in range(3):
        em[k] = mm(mask_ref[k].astype(F32).astype(BF16), spread, 1, 0)

    def prune(k, j):
        w_copy(k, j).wait()

        def one(b, carry):
            i = j * (fc // BLOCK) + b
            keep = jnp.broadcast_to(em[k, pl.ds(i, 1), :], (16, width)).astype(BF16)
            for q in range(BLOCK // 16):
                at = pl.ds(pl.multiple_of(i * BLOCK + q * 16, 16), 16)
                w[k, at, :] = w[k, at, :] * keep
            return carry
        lax.fori_loop(0, fc // BLOCK, one, 0)

    for k in range(3):
        loop(nfc, functools.partial(prune, k))
    for copy in a_copies:
        copy.wait()
    peers(lambda p: ag(p, c).wait_recv())

    def row_copy(i, src, dst):
        return pltpu.make_async_remote_copy(src, dst, row_send.at[i], row_recv.at[i], device_id={"row": 1 - r}, device_id_type=MESH)

    rank_x = row_copy(3, rs, rr)
    pre_x = [row_copy(k, ps.at[k], pr.at[k]) for k in range(3)]

    rs[0] = mm(xg[0], ui[...], 1, 0).astype(BF16)
    rs[1] = mm(xg[1], do[...], 1, 1).astype(BF16)
    rank_x.start()
    for k in range(3):
        def pre(j, k=k):
            ps[k, :, fch(j)] = mm(xg[k // 2], w[k, fch(j), :], 1, 1).astype(BF16)
        loop(nfc, pre)
        pre_x[k].start()

    rank_x.wait_recv()
    for i in range(2):
        ur[i] = (sel[...] * (rs[i].astype(F32) + rr[i].astype(F32))).astype(BF16)
    for k in range(3):
        pre_x[k].wait_recv()

    rk[...] = jnp.zeros_like(rk)

    def middle(j):
        f = fch(j)
        gate = ps[0, :, f].astype(F32) + pr[0, :, f].astype(F32)
        up = ps[1, :, f].astype(F32) + pr[1, :, f].astype(F32) + mm(ur[0], uo[:, f], 1, 0)
        back = ps[2, :, f].astype(F32) + pr[2, :, f].astype(F32) + mm(ur[1], di[f, :], 1, 1)
        s = jax.nn.sigmoid(gate)
        act = gate * s
        hidden = (act * up).astype(BF16)
        grad_up = (back * act).astype(BF16)
        hs[0, :, f] = hidden
        hs[1, :, f] = (back * up * s * (1.0 + gate * (1.0 - s))).astype(BF16)
        hs[2, :, f] = grad_up
        rk[0] += mm(hidden, di[f, :], 1, 0)
        rk[1] += mm(grad_up, uo[:, f], 1, 1)

    loop(nfc, middle)
    rp[...] = rk[...].astype(BF16)

    def rank_copy(owner, p):
        return pltpu.make_async_remote_copy(rp.at[:, rows_of(p)], rrb.at[owner], rank_send.at[p], rank_recv.at[owner], device_id={"col": p}, device_id_type=MESH)

    peers(lambda p: rank_copy(c, p).start())
    rrb[c] = rp[:, mine]

    def share(i, owner, p):
        return pltpu.make_async_remote_copy(ob.at[i, rows_of(p)], rb.at[i, owner], rs_send.at[i, p], rs_recv.at[i, owner], device_id={"col": p}, device_id_type=MESH)

    def dch(j):
        return pl.ds(pl.multiple_of(j * dc, dc), dc)

    def grad_share(j):
        d = dch(j)
        ob[1, :, d] = (mm(hs[1], w[0, :, d], 1, 0) + mm(hs[2], w[1, :, d], 1, 0)).astype(BF16)

    loop(ndc, grad_share)
    peers(lambda p: share(1, c, p).start())
    rb[1, c] = ob[1, mine]

    peers(lambda p: rank_copy(p, c).wait_recv())
    summed = jnp.zeros(rrb.shape[1:], F32)
    summed = lax.fori_loop(0, n, lambda q, acc: acc + rrb[q].astype(F32), summed)
    rg[:, mine] = (sel[mine, :][None] * summed).astype(BF16)

    def rg_copy(owner, p):
        part = rg.at[:, rows_of(owner)]
        return pltpu.make_async_remote_copy(part, part, rg_send.at[p], rg_recv.at[owner], device_id={"col": p}, device_id_type=MESH)

    peers(lambda p: rg_copy(c, p).start())

    def out_share(j):
        d = dch(j)
        ob[0, :, d] = mm(hs[0], w[2, :, d], 1, 0).astype(BF16)

    loop(ndc, out_share)
    peers(lambda p: share(0, c, p).start())
    rb[0, c] = ob[0, mine]

    def local_grads(j):
        f = fch(j)
        guo_ref[:, f] = mm(ur[0], hs[2, :, f], 0, 0).astype(BF16)
        gdi_ref[f, :] = mm(hs[0, :, f], ur[1], 0, 0).astype(BF16)

    loop(nfc, local_grads)
    peers(lambda p: rg_copy(p, c).wait_recv())

    def rank_grads(j):
        d = dch(j)
        gui_ref[d, :] = mm(xg[0, :, d], rg[1], 0, 0).astype(BF16)
        gdo_ref[:, d] = mm(rg[0], xg[1, :, d], 0, 0).astype(BF16)

    loop(ndc, rank_grads)
    peers(lambda p: share(1, p, c).wait_recv())

    def final(i, dest, adapter, contract):
        def step(j):
            d = dch(j)
            total = jnp.zeros((own, dc), F32)
            total = lax.fori_loop(0, n, lambda q, acc: acc + rb[i, q, :, d].astype(F32), total)
            side = adapter[:, d] if contract == 0 else adapter[d, :]
            dest[:, d] = (total + mm(rg[i, mine], side, 1, contract)).astype(BF16)
        loop(ndc, step)

    final(1, tg_ref, ui, 1)
    peers(lambda p: share(0, p, c).wait_recv())
    final(0, out_ref, do, 0)

    rank_x.wait_send()
    for k in range(3):
        pre_x[k].wait_send()

    def drain(p):
        ag(c, p).wait_send()
        rank_copy(c, p).wait_send()
        rg_copy(c, p).wait_send()
        share(0, c, p).wait_send()
        share(1, c, p).wait_send()
    peers(drain)


def per_device(n, tokens, cotangent, adapter_index, retain_mask, gate_weight, up_weight, down_weight, ui, uo, di, do):
    own, width = tokens.shape
    units = gate_weight.shape[0]
    ranks = ui.shape[1]
    group = own * n
    nfc = units // 256 if units % 256 == 0 else 1
    vmem = pl.BlockSpec(memory_space=pltpu.VMEM)
    hbm = pl.BlockSpec(memory_space=pl.ANY)
    dma = pltpu.SemaphoreType.DMA
    V = pltpu.VMEM
    return pl.pallas_call(
        functools.partial(kernel, n),
        out_shape=tuple(
            jax.ShapeDtypeStruct(s, BF16)
            for s in ((own, width), (own, width), (width, ranks), (ranks, units), (units, ranks), (ranks, width))
        ),
        in_specs=[vmem] * 4 + [hbm] * 7,
        out_specs=tuple([vmem] * 6),
        scratch_shapes=[
            V((3, units, width), BF16), V((width, ranks), BF16), V((ranks, units), BF16), V((units, ranks), BF16), V((ranks, width), BF16),
            V((3, units // BLOCK, width), F32), V((group, ranks), F32), V((2, group, width), BF16),
            V((3, group, units), BF16), V((3, group, units), BF16), V((2, group, ranks), BF16), V((2, group, ranks), BF16),
            V((2, group, ranks), BF16), V((2, group, ranks), F32), V((3, group, units), BF16),
            V((2, group, ranks), BF16), V((n, 2, own, ranks), BF16), V((2, group, ranks), BF16),
            V((2, group, width), BF16), V((2, n, own, width), BF16),
            dma((3, nfc)), dma((4,)), dma((n,)), dma((n,)), dma((4,)), dma((4,)), dma((n,)), dma((n,)), dma((n,)), dma((n,)), dma((2, n)), dma((2, n)),
        ],
        compiler_params=pltpu.CompilerParams(collective_id=0, has_side_effects=True, vmem_limit_bytes=58 * 1024 * 1024),
    )(tokens, cotangent, adapter_index.reshape(group, 1), retain_mask, gate_weight, up_weight, down_weight, ui, uo, di, do)


def solution(mesh):
    return jax.shard_map(
        functools.partial(per_device, mesh.shape["col"]),
        mesh=mesh,
        in_specs=(
            P(("grp", "col"), "row"),
            P(("grp", "col"), "row"),
            P("grp"),
            P(None, "col", "row"),
            P("col", "row"),
            P("col", "row"),
            P("col", "row"),
            P("row", None),
            P(None, "col"),
            P("col", None),
            P(None, "row"),
        ),
        out_specs=(
            P(("grp", "col"), "row"),
            P(("grp", "col"), "row"),
            P(("grp", "row"), None),
            P("grp", "col"),
            P(("grp", "col"), None),
            P("grp", "row"),
        ),
        check_vma=False,
    )
```

```python
import functools

import jax
import jax.numpy as jnp
from jax import lax
from jax.experimental import pallas as pl
from jax.experimental.pallas import tpu as pltpu
from jax.sharding import PartitionSpec as P

BLOCK = 64
ADAPTER_RANK = 32
MESH = pl.DeviceIdType.MESH
BF16 = jnp.bfloat16
F32 = jnp.float32


def mm(a, b, ca, cb):
    return lax.dot_general(a, b, (((ca,), (cb,)), ((), ())), preferred_element_type=F32)


def kernel(
    n,
    tok_ref, cot_ref, index_ref, mask_ref, gate_hbm, up_hbm, down_hbm, ui_hbm, uo_hbm, di_hbm, do_hbm,
    out_ref, tg_ref, gui_ref, guo_ref, gdi_ref, gdo_ref,
    w, ui, uo, di, do, em, sel, xg, ps, pr, rs, rr, ur, rk, hs, rp, rrb, rg, ob, ya, s2, rb,
    w_sem, a_sem, ag_send, ag_recv, row_send, row_recv, rank_send, rank_recv, rg_send, rg_recv, ra_send, ra_recv, rs_send, rs_recv,
):
    own = tok_ref.shape[0]
    units, width = gate_hbm.shape
    tokens = own * n
    c = lax.axis_index("col")
    r = lax.axis_index("row")
    half = n // 2
    z, y = c // 2, lax.rem(c, 2)
    other = 1 - y
    partner = 2 * z + other
    fc = 256 if units % 256 == 0 else units
    nfc = units // fc
    dc = 512
    ndc = width // dc

    def rows_of(p):
        return pl.ds(pl.multiple_of(p * own, own), own)

    def fch(j):
        return pl.ds(pl.multiple_of(j * fc, fc), fc) if nfc > 1 else slice(None)

    def peers(body):
        def step(k, carry):
            body(lax.rem(c + k, n))
            return carry
        lax.fori_loop(1, n, step, 0)

    def loop(count, body):
        if count == 1:
            body(0)
        else:
            def step(j, carry):
                body(j)
                return carry
            lax.fori_loop(0, count, step, 0)

    def lines(body, first=1, last=None):
        def step(k, carry):
            body(lax.rem(z + k, half))
            return carry
        lax.fori_loop(first, half if last is None else last, step, 0)

    mine = rows_of(c)

    def w_copy(k, j):
        return pltpu.make_async_copy((gate_hbm, up_hbm, down_hbm)[k].at[fch(j)], w.at[k, fch(j)], w_sem.at[k, j])

    a_copies = [
        pltpu.make_async_copy(src, dst, a_sem.at[i])
        for i, (src, dst) in enumerate(((ui_hbm, ui), (do_hbm, do), (uo_hbm, uo), (di_hbm, di)))
    ]
    for k in range(3):
        loop(nfc, lambda j, k=k: w_copy(k, j).start())
        if k == 0:
            for copy in a_copies:
                copy.start()

    barrier = pltpu.get_barrier_semaphore()
    peers(lambda p: pl.semaphore_signal(barrier, inc=1, device_id={"col": p}, device_id_type=MESH))
    pl.semaphore_signal(barrier, inc=1, device_id={"row": 1 - r}, device_id_type=MESH)
    xg[0, mine] = tok_ref[...]
    xg[1, mine] = cot_ref[...]
    pl.semaphore_wait(barrier, n)

    def ag(owner, p, slot):
        part = xg.at[:, rows_of(owner)]
        return pltpu.make_async_remote_copy(part, part, ag_send.at[slot], ag_recv.at[owner], device_id={"col": p}, device_id_type=MESH)

    lines(lambda q: ag(c, 2 * q + y, 2 * q + y).start())
    ag(c, partner, partner).start()

    def forward(q):
        ag(2 * q + y, c, c).wait_recv()
        ag(2 * q + y, partner, 2 * q + other).start()

    member = lax.broadcasted_iota(jnp.int32, (sel.shape[1], tokens), 0) // ADAPTER_RANK
    sel[...] = jnp.where(index_ref[...] == member, 1.0, 0.0).astype(F32).T
    blocks = mask_ref.shape[2]
    spread = (
        lax.broadcasted_iota(jnp.int32, (blocks, width), 1) // BLOCK
        == lax.broadcasted_iota(jnp.int32, (blocks, width), 0)
    ).astype(F32).astype(BF16)
    for k in range(3):
        em[k] = mm(mask_ref[k].astype(F32).astype(BF16), spread, 1, 0)

    def prune(k, j):
        w_copy(k, j).wait()

        def one(b, carry):
            i = j * (fc // BLOCK) + b
            keep = jnp.broadcast_to(em[k, pl.ds(i, 1), :], (16, width)).astype(BF16)
            for q in range(BLOCK // 16):
                at = pl.ds(pl.multiple_of(i * BLOCK + q * 16, 16), 16)
                w[k, at, :] = w[k, at, :] * keep
            return carry
        lax.fori_loop(0, fc // BLOCK, one, 0)

    for k in range(3):
        loop(nfc, functools.partial(prune, k))
        lines(forward, 1 + (half - 1) * k // 3, 1 + (half - 1) * (k + 1) // 3)
    for copy in a_copies:
        copy.wait()
    ag(partner, c, c).wait_recv()
    lines(lambda q: ag(2 * q + other, c, c).wait_recv())

    def row_copy(i, src, dst):
        return pltpu.make_async_remote_copy(src, dst, row_send.at[i], row_recv.at[i], device_id={"row": 1 - r}, device_id_type=MESH)

    rank_x = row_copy(nfc, rs, rr)

    def pre_x(j):
        return row_copy(j, ps.at[:, :, fch(j)], pr.at[:, :, fch(j)])

    rs[0] = mm(xg[0], ui[...], 1, 0).astype(BF16)
    rs[1] = mm(xg[1], do[...], 1, 1).astype(BF16)
    rank_x.start()
    def pre(j):
        for k in range(3):
            ps[k, :, fch(j)] = mm(xg[k // 2], w[k, fch(j), :], 1, 1).astype(BF16)
        pre_x(j).start()

    loop(nfc, pre)
    rank_x.wait_recv()
    for i in range(2):
        ur[i] = (sel[...] * (rs[i].astype(F32) + rr[i].astype(F32))).astype(BF16)
    rk[...] = jnp.zeros_like(rk)

    def middle(j):
        f = fch(j)
        pre_x(j).wait_recv()
        gate = ps[0, :, f].astype(F32) + pr[0, :, f].astype(F32)
        up = ps[1, :, f].astype(F32) + pr[1, :, f].astype(F32) + mm(ur[0], uo[:, f], 1, 0)
        back = ps[2, :, f].astype(F32) + pr[2, :, f].astype(F32) + mm(ur[1], di[f, :], 1, 1)
        s = jax.nn.sigmoid(gate)
        act = gate * s
        hidden = (act * up).astype(BF16)
        grad_up = (back * act).astype(BF16)
        hs[0, :, f] = hidden
        hs[1, :, f] = (back * up * s * (1.0 + gate * (1.0 - s))).astype(BF16)
        hs[2, :, f] = grad_up
        rk[0] += mm(hidden, di[f, :], 1, 0)
        rk[1] += mm(grad_up, uo[:, f], 1, 1)

    loop(nfc, middle)
    rp[...] = rk[...].astype(BF16)

    def rank_copy(owner, p):
        return pltpu.make_async_remote_copy(rp.at[:, rows_of(p)], rrb.at[owner], rank_send.at[p], rank_recv.at[owner], device_id={"col": p}, device_id_type=MESH)

    peers(lambda p: rank_copy(c, p).start())
    rrb[c] = rp[:, mine]

    def to_partner(i, q):
        return pltpu.make_async_remote_copy(ob.at[i, rows_of(2 * q + other)], ya.at[i, q], ra_send.at[i, q], ra_recv.at[i, q], device_id={"col": partner}, device_id_type=MESH)

    def along(i, q, owner):
        return pltpu.make_async_remote_copy(s2.at[i, q], rb.at[i, owner], rs_send.at[i, q], rs_recv.at[i, owner], device_id={"col": 2 * q + y}, device_id_type=MESH)

    def first_hop(i):
        lines(lambda q: to_partner(i, q).start())
        to_partner(i, z).start()

    def pair_sum(i, q):
        to_partner(i, q).wait_recv()
        return (ob[i, rows_of(2 * q + y)].astype(F32) + ya[i, q].astype(F32)).astype(BF16)

    def second_hop(i):
        def go(q):
            s2[i, q] = pair_sum(i, q)
            along(i, q, z).start()
        lines(go)
        rb[i, z] = pair_sum(i, z)

    def dch(j):
        return pl.ds(pl.multiple_of(j * dc, dc), dc)

    def grad_share(j):
        d = dch(j)
        ob[1, :, d] = (mm(hs[1], w[0, :, d], 1, 0) + mm(hs[2], w[1, :, d], 1, 0)).astype(BF16)

    def out_share(j):
        d = dch(j)
        ob[0, :, d] = mm(hs[0], w[2, :, d], 1, 0).astype(BF16)

    loop(ndc, out_share)
    first_hop(0)
    peers(lambda p: rank_copy(p, c).wait_recv())
    summed = jnp.zeros(rrb.shape[1:], F32)
    summed = lax.fori_loop(0, n, lambda q, acc: acc + rrb[q].astype(F32), summed)
    rg[:, mine] = (sel[mine, :][None] * summed).astype(BF16)

    def rg_copy(owner, p):
        part = rg.at[:, rows_of(owner)]
        return pltpu.make_async_remote_copy(part, part, rg_send.at[p], rg_recv.at[owner], device_id={"col": p}, device_id_type=MESH)

    peers(lambda p: rg_copy(c, p).start())

    loop(ndc, grad_share)
    first_hop(1)
    second_hop(0)

    def local_grads(j):
        f = fch(j)
        guo_ref[:, f] = mm(ur[0], hs[2, :, f], 0, 0).astype(BF16)
        gdi_ref[f, :] = mm(hs[0, :, f], ur[1], 0, 0).astype(BF16)

    loop(nfc, local_grads)
    second_hop(1)
    peers(lambda p: rg_copy(p, c).wait_recv())

    def rank_grads(j):
        d = dch(j)
        gui_ref[d, :] = mm(xg[0, :, d], rg[1], 0, 0).astype(BF16)
        gdo_ref[:, d] = mm(rg[0], xg[1, :, d], 0, 0).astype(BF16)

    loop(ndc, rank_grads)

    def final(i, dest, adapter, contract):
        def step(j):
            d = dch(j)
            total = jnp.zeros((own, dc), F32)
            total = lax.fori_loop(0, half, lambda q, acc: acc + rb[i, q, :, d].astype(F32), total)
            side = adapter[:, d] if contract == 0 else adapter[d, :]
            dest[:, d] = (total + mm(rg[i, mine], side, 1, contract)).astype(BF16)
        loop(ndc, step)

    lines(lambda q: along(0, z, q).wait_recv())
    final(0, out_ref, do, 0)
    lines(lambda q: along(1, z, q).wait_recv())
    final(1, tg_ref, ui, 1)

    rank_x.wait_send()
    loop(nfc, lambda j: pre_x(j).wait_send())
    ag(c, partner, partner).wait_send()

    def drain_lines(q):
        ag(c, 2 * q + y, 2 * q + y).wait_send()
        ag(2 * q + y, partner, 2 * q + other).wait_send()
        for i in range(2):
            to_partner(i, q).wait_send()
            along(i, q, z).wait_send()
    lines(drain_lines)
    for i in range(2):
        to_partner(i, z).wait_send()

    def drain(p):
        rank_copy(c, p).wait_send()
        rg_copy(c, p).wait_send()
    peers(drain)


def store(*refs):
    count = len(refs) // 2
    sems = refs[-1]
    copies = [pltpu.make_async_copy(refs[i], refs[count + i], sems.at[i]) for i in range(count)]
    for copy in copies:
        copy.start()
    for copy in copies:
        copy.wait()


def per_device(n, tokens, cotangent, adapter_index, retain_mask, gate_weight, up_weight, down_weight, ui, uo, di, do):
    own, width = tokens.shape
    units = gate_weight.shape[0]
    ranks = ui.shape[1]
    group = own * n
    nfc = units // 256 if units % 256 == 0 else 1
    vmem = pl.BlockSpec(memory_space=pltpu.VMEM)
    hbm = pl.BlockSpec(memory_space=pl.ANY)
    dma = pltpu.SemaphoreType.DMA
    V = pltpu.VMEM
    shapes = tuple(
        jax.ShapeDtypeStruct(s, BF16)
        for s in ((own, width), (own, width), (width, ranks), (ranks, units), (units, ranks), (ranks, width))
    )
    held = pl.pallas_call(
        functools.partial(kernel, n),
        out_shape=tuple(V(s.shape, BF16) for s in shapes),
        in_specs=[vmem] * 4 + [hbm] * 7,
        out_specs=tuple([vmem] * 6),
        scratch_shapes=[
            V((3, units, width), BF16), V((width, ranks), BF16), V((ranks, units), BF16), V((units, ranks), BF16), V((ranks, width), BF16),
            V((3, units // BLOCK, width), F32), V((group, ranks), F32), V((2, group, width), BF16),
            V((3, group, units), BF16), V((3, group, units), BF16), V((2, group, ranks), BF16), V((2, group, ranks), BF16),
            V((2, group, ranks), BF16), V((2, group, ranks), F32), V((3, group, units), BF16),
            V((2, group, ranks), BF16), V((n, 2, own, ranks), BF16), V((2, group, ranks), BF16),
            V((2, group, width), BF16), V((2, n // 2, own, width), BF16), V((2, n // 2, own, width), BF16), V((2, n // 2, own, width), BF16),
            dma((3, nfc)), dma((4,)), dma((n,)), dma((n,)), dma((nfc + 1,)), dma((nfc + 1,)), dma((n,)), dma((n,)), dma((n,)), dma((n,)),
            dma((2, n // 2)), dma((2, n // 2)), dma((2, n // 2)), dma((2, n // 2)),
        ],
        compiler_params=pltpu.CompilerParams(collective_id=0, has_side_effects=True, vmem_limit_bytes=50 * 1024 * 1024),
    )(tokens, cotangent, adapter_index.reshape(1, group), retain_mask, gate_weight, up_weight, down_weight, ui, uo, di, do)
    return pl.pallas_call(
        store,
        out_shape=shapes,
        in_specs=[vmem] * 6,
        out_specs=tuple([hbm] * 6),
        scratch_shapes=[dma((6,))],
        compiler_params=pltpu.CompilerParams(vmem_limit_bytes=8 * 1024 * 1024),
    )(*(pltpu.with_memory_space_constraint(x, pltpu.VMEM) for x in held))


def solution(mesh):
    return jax.shard_map(
        functools.partial(per_device, mesh.shape["col"]),
        mesh=mesh,
        in_specs=(
            P(("grp", "col"), "row"),
            P(("grp", "col"), "row"),
            P("grp"),
            P(None, "col", "row"),
            P("col", "row"),
            P("col", "row"),
            P("col", "row"),
            P("row", None),
            P(None, "col"),
            P("col", None),
            P(None, "row"),
        ),
        out_specs=(
            P(("grp", "col"), "row"),
            P(("grp", "col"), "row"),
            P(("grp", "row"), None),
            P("grp", "col"),
            P(("grp", "col"), None),
            P("grp", "row"),
        ),
        check_vma=False,
    )
```

```python
import functools

import jax
import jax.numpy as jnp
from jax import lax
from jax.experimental import pallas as pl
from jax.experimental.pallas import tpu as pltpu
from jax.sharding import PartitionSpec as P

BLOCK = 64
ADAPTER_RANK = 32
MESH = pl.DeviceIdType.MESH
BF16 = jnp.bfloat16
F32 = jnp.float32


def mm(a, b, ca, cb):
    return lax.dot_general(a, b, (((ca,), (cb,)), ((), ())), preferred_element_type=F32)


def kernel(
    n,
    tok_ref, cot_ref, index_ref, mask_ref, gate_hbm, up_hbm, down_hbm, ui_hbm, uo_hbm, di_hbm, do_hbm,
    out_ref, tg_ref, gui_ref, guo_ref, gdi_ref, gdo_ref,
    w, ui, uo, di, do, em, sel, xg, ps, pr, rs, rr, ur, rk, hs, rp, rrb, rg, ob, ya, s2, rb,
    w_sem, a_sem, ag_send, ag_recv, row_send, row_recv, rank_send, rank_recv, rg_send, rg_recv, ra_send, ra_recv, rs_send, rs_recv,
):
    own = tok_ref.shape[0]
    units, width = gate_hbm.shape
    tokens = own * n
    c = lax.axis_index("col")
    r = lax.axis_index("row")
    half = n // 2
    z, y = c // 2, lax.rem(c, 2)
    other = 1 - y
    partner = 2 * z + other
    fc = 256 if units % 256 == 0 else units
    nfc = units // fc
    dc = 512
    ndc = width // dc
    npc = ndc // 2

    def rows_of(p):
        return pl.ds(pl.multiple_of(p * own, own), own)

    def fch(j):
        return pl.ds(pl.multiple_of(j * fc, fc), fc) if nfc > 1 else slice(None)

    def peers(body):
        def step(k, carry):
            body(lax.rem(c + k, n))
            return carry
        lax.fori_loop(1, n, step, 0)

    def loop(count, body):
        if count == 1:
            body(0)
        else:
            def step(j, carry):
                body(j)
                return carry
            lax.fori_loop(0, count, step, 0)

    def lines(body, first=1, last=None):
        def step(k, carry):
            body(lax.rem(z + k, half))
            return carry
        lax.fori_loop(first, half if last is None else last, step, 0)

    mine = rows_of(c)

    def w_copy(k, j):
        return pltpu.make_async_copy((gate_hbm, up_hbm, down_hbm)[k].at[fch(j)], w.at[k, fch(j)], w_sem.at[k, j])

    a_copies = [
        pltpu.make_async_copy(src, dst, a_sem.at[i])
        for i, (src, dst) in enumerate(((ui_hbm, ui), (do_hbm, do), (uo_hbm, uo), (di_hbm, di)))
    ]
    for k in range(3):
        loop(nfc, lambda j, k=k: w_copy(k, j).start())
        if k == 0:
            for copy in a_copies:
                copy.start()

    barrier = pltpu.get_barrier_semaphore()
    peers(lambda p: pl.semaphore_signal(barrier, inc=1, device_id={"col": p}, device_id_type=MESH))
    pl.semaphore_signal(barrier, inc=1, device_id={"row": 1 - r}, device_id_type=MESH)
    xg[0, mine] = tok_ref[...]
    xg[1, mine] = cot_ref[...]
    pl.semaphore_wait(barrier, n)

    def ag(i, owner, p, slot):
        part = xg.at[i, rows_of(owner)]
        return pltpu.make_async_remote_copy(part, part, ag_send.at[i, slot], ag_recv.at[i, owner], device_id={"col": p}, device_id_type=MESH)

    for i in range(2):
        lines(lambda q, i=i: ag(i, c, 2 * q + y, 2 * q + y).start())
        ag(i, c, partner, partner).start()

    def forward(i, part, parts):
        def go(q):
            ag(i, 2 * q + y, c, c).wait_recv()
            ag(i, 2 * q + y, partner, 2 * q + other).start()
        lines(go, 1 + (half - 1) * part // parts, 1 + (half - 1) * (part + 1) // parts)

    def arrive(i):
        ag(i, partner, c, c).wait_recv()
        lines(lambda q: ag(i, 2 * q + other, c, c).wait_recv())

    member = lax.broadcasted_iota(jnp.int32, (sel.shape[1], tokens), 0) // ADAPTER_RANK
    sel[...] = jnp.where(index_ref[...] == member, 1.0, 0.0).astype(F32).T
    blocks = mask_ref.shape[2]
    spread = (
        lax.broadcasted_iota(jnp.int32, (blocks, width), 1) // BLOCK
        == lax.broadcasted_iota(jnp.int32, (blocks, width), 0)
    ).astype(F32).astype(BF16)
    for k in range(3):
        em[k] = mm(mask_ref[k].astype(F32).astype(BF16), spread, 1, 0)

    def prune(k, j):
        w_copy(k, j).wait()

        def one(b, carry):
            i = j * (fc // BLOCK) + b
            keep = jnp.broadcast_to(em[k, pl.ds(i, 1), :], (16, width)).astype(BF16)
            for q in range(BLOCK // 16):
                at = pl.ds(pl.multiple_of(i * BLOCK + q * 16, 16), 16)
                w[k, at, :] = w[k, at, :] * keep
            return carry
        lax.fori_loop(0, fc // BLOCK, one, 0)

    def row_copy(i, src, dst):
        return pltpu.make_async_remote_copy(src, dst, row_send.at[i], row_recv.at[i], device_id={"row": 1 - r}, device_id_type=MESH)

    rank_x = row_copy(3 * nfc, rs, rr)

    def pre_x(k, j):
        return row_copy(k * nfc + j, ps.at[k, :, fch(j)], pr.at[k, :, fch(j)])

    def pre(k, j):
        ps[k, :, fch(j)] = mm(xg[k // 2], w[k, fch(j), :], 1, 1).astype(BF16)
        pre_x(k, j).start()

    loop(nfc, functools.partial(prune, 0))
    forward(0, 0, 2)
    loop(nfc, functools.partial(prune, 1))
    forward(0, 1, 2)
    for copy in a_copies:
        copy.wait()
    arrive(0)
    loop(nfc, functools.partial(pre, 0))
    forward(1, 0, 2)
    loop(nfc, functools.partial(prune, 2))
    forward(1, 1, 2)
    loop(nfc, functools.partial(pre, 1))
    rs[0] = mm(xg[0], ui[...], 1, 0).astype(BF16)
    arrive(1)
    rs[1] = mm(xg[1], do[...], 1, 1).astype(BF16)
    rank_x.start()
    loop(nfc, functools.partial(pre, 2))

    rank_x.wait_recv()
    for i in range(2):
        ur[i] = (sel[...] * (rs[i].astype(F32) + rr[i].astype(F32))).astype(BF16)
    rk[...] = jnp.zeros_like(rk)

    def middle(j):
        f = fch(j)
        for k in range(3):
            pre_x(k, j).wait_recv()
        gate = ps[0, :, f].astype(F32) + pr[0, :, f].astype(F32)
        up = ps[1, :, f].astype(F32) + pr[1, :, f].astype(F32) + mm(ur[0], uo[:, f], 1, 0)
        back = ps[2, :, f].astype(F32) + pr[2, :, f].astype(F32) + mm(ur[1], di[f, :], 1, 1)
        s = jax.nn.sigmoid(gate)
        act = gate * s
        hidden = (act * up).astype(BF16)
        grad_up = (back * act).astype(BF16)
        hs[0, :, f] = hidden
        hs[1, :, f] = (back * up * s * (1.0 + gate * (1.0 - s))).astype(BF16)
        hs[2, :, f] = grad_up
        rk[0] += mm(hidden, di[f, :], 1, 0)
        rk[1] += mm(grad_up, uo[:, f], 1, 1)

    loop(nfc, middle)
    rp[...] = rk[...].astype(BF16)

    def rank_copy(owner, p):
        return pltpu.make_async_remote_copy(rp.at[:, rows_of(p)], rrb.at[owner], rank_send.at[p], rank_recv.at[owner], device_id={"col": p}, device_id_type=MESH)

    peers(lambda p: rank_copy(c, p).start())
    rrb[c] = rp[:, mine]

    def to_partner(i, q):
        return pltpu.make_async_remote_copy(ob.at[i, rows_of(2 * q + other)], ya.at[i, q], ra_send.at[i, q], ra_recv.at[i, q], device_id={"col": partner}, device_id_type=MESH)

    def along(i, q, owner):
        return pltpu.make_async_remote_copy(s2.at[i, q], rb.at[i, owner], rs_send.at[i, q], rs_recv.at[i, owner], device_id={"col": 2 * q + y}, device_id_type=MESH)

    def first_hop(i):
        lines(lambda q: to_partner(i, q).start())
        to_partner(i, z).start()

    def pair_sum(i, q):
        to_partner(i, q).wait_recv()
        return (ob[i, rows_of(2 * q + y)].astype(F32) + ya[i, q].astype(F32)).astype(BF16)

    def second_hop(i):
        def go(q):
            s2[i, q] = pair_sum(i, q)
            along(i, q, z).start()
        lines(go)
        rb[i, z] = pair_sum(i, z)

    def dch(j):
        return pl.ds(pl.multiple_of(j * dc, dc), dc)

    def part_share(i):
        def step(j):
            d, local = dch(j + (i % 2) * npc), dch(j)
            if i < 2:
                term = mm(hs[0], w[2, :, d], 1, 0)
            else:
                term = mm(hs[1], w[0, :, d], 1, 0) + mm(hs[2], w[1, :, d], 1, 0)
            ob[i, :, local] = term.astype(BF16)
        loop(npc, step)
        first_hop(i)

    part_share(0)
    part_share(1)

    peers(lambda p: rank_copy(p, c).wait_recv())
    summed = jnp.zeros(rrb.shape[1:], F32)
    summed = lax.fori_loop(0, n, lambda q, acc: acc + rrb[q].astype(F32), summed)
    rg[:, mine] = (sel[mine, :][None] * summed).astype(BF16)

    def rg_copy(owner, p):
        part = rg.at[:, rows_of(owner)]
        return pltpu.make_async_remote_copy(part, part, rg_send.at[p], rg_recv.at[owner], device_id={"col": p}, device_id_type=MESH)

    peers(lambda p: rg_copy(c, p).start())

    part_share(2)
    second_hop(0)
    part_share(3)
    second_hop(1)

    def local_grads(j):
        f = fch(j)
        guo_ref[:, f] = mm(ur[0], hs[2, :, f], 0, 0).astype(BF16)
        gdi_ref[f, :] = mm(hs[0, :, f], ur[1], 0, 0).astype(BF16)

    loop(nfc, local_grads)
    second_hop(2)
    peers(lambda p: rg_copy(p, c).wait_recv())

    def rank_grads(j):
        d = dch(j)
        gui_ref[d, :] = mm(xg[0, :, d], rg[1], 0, 0).astype(BF16)
        gdo_ref[:, d] = mm(rg[0], xg[1, :, d], 0, 0).astype(BF16)

    loop(ndc, rank_grads)
    second_hop(3)

    def final(i, dest, adapter, contract):
        lines(lambda q: along(i, z, q).wait_recv())
        for j in range(npc):
            d, local = pl.ds((j + (i % 2) * npc) * dc, dc), pl.ds(j * dc, dc)
            total = jnp.zeros((own, dc), F32)
            total = lax.fori_loop(0, half, lambda q, acc, local=local: acc + rb[i, q, :, local].astype(F32), total)
            side = adapter[:, d] if contract == 0 else adapter[d, :]
            dest[:, d] = (total + mm(rg[i // 2, mine], side, 1, contract)).astype(BF16)

    for i in range(4):
        final(i, (out_ref, tg_ref)[i // 2], (do, ui)[i // 2], i // 2)

    rank_x.wait_send()
    for k in range(3):
        loop(nfc, lambda j, k=k: pre_x(k, j).wait_send())
    for i in range(2):
        ag(i, c, partner, partner).wait_send()

    def drain_lines(q):
        for i in range(2):
            ag(i, c, 2 * q + y, 2 * q + y).wait_send()
            ag(i, 2 * q + y, partner, 2 * q + other).wait_send()
        for i in range(4):
            to_partner(i, q).wait_send()
            along(i, q, z).wait_send()
    lines(drain_lines)
    for i in range(4):
        to_partner(i, z).wait_send()

    def drain(p):
        rank_copy(c, p).wait_send()
        rg_copy(c, p).wait_send()
    peers(drain)


def store(*refs):
    count = len(refs) // 2
    sems = refs[-1]
    copies = [pltpu.make_async_copy(refs[i], refs[count + i], sems.at[i]) for i in range(count)]
    for copy in copies:
        copy.start()
    for copy in copies:
        copy.wait()


def per_device(n, tokens, cotangent, adapter_index, retain_mask, gate_weight, up_weight, down_weight, ui, uo, di, do):
    own, width = tokens.shape
    units = gate_weight.shape[0]
    ranks = ui.shape[1]
    group = own * n
    nfc = units // 256 if units % 256 == 0 else 1
    vmem = pl.BlockSpec(memory_space=pltpu.VMEM)
    hbm = pl.BlockSpec(memory_space=pl.ANY)
    dma = pltpu.SemaphoreType.DMA
    V = pltpu.VMEM
    shapes = tuple(
        jax.ShapeDtypeStruct(s, BF16)
        for s in ((own, width), (own, width), (width, ranks), (ranks, units), (units, ranks), (ranks, width))
    )
    held = pl.pallas_call(
        functools.partial(kernel, n),
        out_shape=tuple(V(s.shape, BF16) for s in shapes),
        in_specs=[vmem] * 4 + [hbm] * 7,
        out_specs=tuple([vmem] * 6),
        scratch_shapes=[
            V((3, units, width), BF16), V((width, ranks), BF16), V((ranks, units), BF16), V((units, ranks), BF16), V((ranks, width), BF16),
            V((3, units // BLOCK, width), F32), V((group, ranks), F32), V((2, group, width), BF16),
            V((3, group, units), BF16), V((3, group, units), BF16), V((2, group, ranks), BF16), V((2, group, ranks), BF16),
            V((2, group, ranks), BF16), V((2, group, ranks), F32), V((3, group, units), BF16),
            V((2, group, ranks), BF16), V((n, 2, own, ranks), BF16), V((2, group, ranks), BF16),
            V((4, group, width // 2), BF16), V((4, n // 2, own, width // 2), BF16), V((4, n // 2, own, width // 2), BF16), V((4, n // 2, own, width // 2), BF16),
            dma((3, nfc)), dma((4,)), dma((2, n)), dma((2, n)), dma((3 * nfc + 1,)), dma((3 * nfc + 1,)), dma((n,)), dma((n,)), dma((n,)), dma((n,)),
            dma((4, n // 2)), dma((4, n // 2)), dma((4, n // 2)), dma((4, n // 2)),
        ],
        compiler_params=pltpu.CompilerParams(collective_id=0, has_side_effects=True, vmem_limit_bytes=50 * 1024 * 1024),
    )(tokens, cotangent, adapter_index.reshape(1, group), retain_mask, gate_weight, up_weight, down_weight, ui, uo, di, do)
    return pl.pallas_call(
        store,
        out_shape=shapes,
        in_specs=[vmem] * 6,
        out_specs=tuple([hbm] * 6),
        scratch_shapes=[dma((6,))],
        compiler_params=pltpu.CompilerParams(vmem_limit_bytes=8 * 1024 * 1024),
    )(*(pltpu.with_memory_space_constraint(x, pltpu.VMEM) for x in held))


def solution(mesh):
    return jax.shard_map(
        functools.partial(per_device, mesh.shape["col"]),
        mesh=mesh,
        in_specs=(
            P(("grp", "col"), "row"),
            P(("grp", "col"), "row"),
            P("grp"),
            P(None, "col", "row"),
            P("col", "row"),
            P("col", "row"),
            P("col", "row"),
            P("row", None),
            P(None, "col"),
            P("col", None),
            P(None, "row"),
        ),
        out_specs=(
            P(("grp", "col"), "row"),
            P(("grp", "col"), "row"),
            P(("grp", "row"), None),
            P("grp", "col"),
            P(("grp", "col"), None),
            P("grp", "row"),
        ),
        check_vma=False,
    )
```

```python
import functools

import jax
import jax.numpy as jnp
from jax import lax
from jax.experimental import pallas as pl
from jax.experimental.pallas import tpu as pltpu
from jax.sharding import PartitionSpec as P

BLOCK = 64
ADAPTER_RANK = 32
MESH = pl.DeviceIdType.MESH
BF16 = jnp.bfloat16
F32 = jnp.float32


def mm(a, b, ca, cb):
    return lax.dot_general(a, b, (((ca,), (cb,)), ((), ())), preferred_element_type=F32)


def kernel(
    n,
    tok_ref, cot_ref, index_ref, mask_ref, gate_hbm, up_hbm, down_hbm, ui_hbm, uo_hbm, di_hbm, do_hbm,
    out_ref, tg_ref, gui_ref, guo_ref, gdi_ref, gdo_ref,
    w, ui, uo, di, do, em, sel, xg, ps, pr, rs, rr, ur, rk, hs, rp, rrb, rg, ob, ya, s2, rb,
    w_sem, a_sem, ag_send, ag_recv, row_send, row_recv, rank_send, rank_recv, rg_send, rg_recv, ra_send, ra_recv, rs_send, rs_recv,
):
    own = tok_ref.shape[0]
    units, width = gate_hbm.shape
    tokens = own * n
    c = lax.axis_index("col")
    r = lax.axis_index("row")
    half = n // 2
    z, y = c // 2, lax.rem(c, 2)
    other = 1 - y
    partner = 2 * z + other
    fc = 256 if units % 256 == 0 else units
    nfc = units // fc
    dc = 512
    ndc = width // dc
    npc = ndc // 2

    def rows_of(p):
        return pl.ds(pl.multiple_of(p * own, own), own)

    def fch(j):
        return pl.ds(pl.multiple_of(j * fc, fc), fc) if nfc > 1 else slice(None)

    def peers(body):
        def step(k, carry):
            body(lax.rem(c + k, n))
            return carry
        lax.fori_loop(1, n, step, 0)

    def loop(count, body):
        if count == 1:
            body(0)
        else:
            def step(j, carry):
                body(j)
                return carry
            lax.fori_loop(0, count, step, 0)

    def lines(body, first=1, last=None):
        def step(k, carry):
            body(lax.rem(z + k, half))
            return carry
        lax.fori_loop(first, half if last is None else last, step, 0)

    mine = rows_of(c)

    def w_copy(k, j):
        return pltpu.make_async_copy((gate_hbm, up_hbm, down_hbm)[k].at[fch(j)], w.at[k, fch(j)], w_sem.at[k, j])

    a_copies = [
        pltpu.make_async_copy(src, dst, a_sem.at[i])
        for i, (src, dst) in enumerate(((ui_hbm, ui), (do_hbm, do), (uo_hbm, uo), (di_hbm, di)))
    ]
    for k in range(3):
        loop(nfc, lambda j, k=k: w_copy(k, j).start())
        if k == 0:
            for copy in a_copies:
                copy.start()

    barrier = pltpu.get_barrier_semaphore()
    peers(lambda p: pl.semaphore_signal(barrier, inc=1, device_id={"col": p}, device_id_type=MESH))
    pl.semaphore_signal(barrier, inc=1, device_id={"row": 1 - r}, device_id_type=MESH)
    xg[0, mine] = tok_ref[...]
    xg[1, mine] = cot_ref[...]
    pl.semaphore_wait(barrier, n)

    def ag(i, owner, p, slot):
        part = xg.at[i, rows_of(owner)]
        return pltpu.make_async_remote_copy(part, part, ag_send.at[i, slot], ag_recv.at[i, owner], device_id={"col": p}, device_id_type=MESH)

    for i in range(2):
        lines(lambda q, i=i: ag(i, c, 2 * q + y, 2 * q + y).start())
        ag(i, c, partner, partner).start()

    def forward(i, part, parts):
        def go(q):
            ag(i, 2 * q + y, c, c).wait_recv()
            ag(i, 2 * q + y, partner, 2 * q + other).start()
        lines(go, 1 + (half - 1) * part // parts, 1 + (half - 1) * (part + 1) // parts)

    def arrive(i):
        ag(i, partner, c, c).wait_recv()
        lines(lambda q: ag(i, 2 * q + other, c, c).wait_recv())

    member = lax.broadcasted_iota(jnp.int32, (sel.shape[1], tokens), 0) // ADAPTER_RANK
    sel[...] = jnp.where(index_ref[...] == member, 1.0, 0.0).astype(F32).T
    blocks = mask_ref.shape[2]
    spread = (
        lax.broadcasted_iota(jnp.int32, (blocks, width), 1) // BLOCK
        == lax.broadcasted_iota(jnp.int32, (blocks, width), 0)
    ).astype(F32).astype(BF16)
    for k in range(3):
        em[k] = mm(mask_ref[k].astype(F32).astype(BF16), spread, 1, 0)

    def prune(k, j):
        w_copy(k, j).wait()

        def one(b, carry):
            i = j * (fc // BLOCK) + b
            keep = jnp.broadcast_to(em[k, pl.ds(i, 1), :], (16, width)).astype(BF16)
            for q in range(BLOCK // 16):
                at = pl.ds(pl.multiple_of(i * BLOCK + q * 16, 16), 16)
                w[k, at, :] = w[k, at, :] * keep
            return carry
        lax.fori_loop(0, fc // BLOCK, one, 0)

    def row_copy(i, src, dst):
        return pltpu.make_async_remote_copy(src, dst, row_send.at[i], row_recv.at[i], device_id={"row": 1 - r}, device_id_type=MESH)

    rank_x = row_copy(3 * nfc, rs, rr)

    def pre_x(k, j):
        return row_copy(k * nfc + j, ps.at[k, :, fch(j)], pr.at[k, :, fch(j)])

    def pre(k, j):
        ps[k, :, fch(j)] = mm(xg[k // 2], w[k, fch(j), :], 1, 1).astype(BF16)
        pre_x(k, j).start()

    forward(0, 0, 2)
    loop(nfc, functools.partial(prune, 0))
    forward(0, 1, 2)
    loop(nfc, functools.partial(prune, 1))
    for copy in a_copies:
        copy.wait()
    forward(1, 0, 2)
    arrive(0)
    loop(nfc, functools.partial(pre, 0))
    forward(1, 1, 2)
    loop(nfc, functools.partial(prune, 2))
    loop(nfc, functools.partial(pre, 1))
    rs[0] = mm(xg[0], ui[...], 1, 0).astype(BF16)
    arrive(1)
    rs[1] = mm(xg[1], do[...], 1, 1).astype(BF16)
    rank_x.start()
    loop(nfc, functools.partial(pre, 2))

    rank_x.wait_recv()
    for i in range(2):
        ur[i] = (sel[...] * (rs[i].astype(F32) + rr[i].astype(F32))).astype(BF16)
    rk[...] = jnp.zeros_like(rk)

    def middle(j):
        f = fch(j)
        for k in range(3):
            pre_x(k, j).wait_recv()
        gate = ps[0, :, f].astype(F32) + pr[0, :, f].astype(F32)
        up = ps[1, :, f].astype(F32) + pr[1, :, f].astype(F32) + mm(ur[0], uo[:, f], 1, 0)
        back = ps[2, :, f].astype(F32) + pr[2, :, f].astype(F32) + mm(ur[1], di[f, :], 1, 1)
        s = jax.nn.sigmoid(gate)
        act = gate * s
        hidden = (act * up).astype(BF16)
        grad_up = (back * act).astype(BF16)
        hs[0, :, f] = hidden
        hs[1, :, f] = (back * up * s * (1.0 + gate * (1.0 - s))).astype(BF16)
        hs[2, :, f] = grad_up
        rk[0] += mm(hidden, di[f, :], 1, 0)
        rk[1] += mm(grad_up, uo[:, f], 1, 1)

    loop(nfc, middle)
    rp[...] = rk[...].astype(BF16)

    def rank_copy(owner, p):
        return pltpu.make_async_remote_copy(rp.at[:, rows_of(p)], rrb.at[owner], rank_send.at[p], rank_recv.at[owner], device_id={"col": p}, device_id_type=MESH)

    peers(lambda p: rank_copy(c, p).start())
    rrb[c] = rp[:, mine]

    def to_partner(i, q):
        return pltpu.make_async_remote_copy(ob.at[i, rows_of(2 * q + other)], ya.at[i, q], ra_send.at[i, q], ra_recv.at[i, q], device_id={"col": partner}, device_id_type=MESH)

    def along(i, q, owner):
        return pltpu.make_async_remote_copy(s2.at[i, q], rb.at[i, owner], rs_send.at[i, q], rs_recv.at[i, owner], device_id={"col": 2 * q + y}, device_id_type=MESH)

    def first_hop(i):
        lines(lambda q: to_partner(i, q).start())
        to_partner(i, z).start()

    def pair_sum(i, q):
        to_partner(i, q).wait_recv()
        return (ob[i, rows_of(2 * q + y)].astype(F32) + ya[i, q].astype(F32)).astype(BF16)

    def second_hop(i):
        def go(q):
            s2[i, q] = pair_sum(i, q)
            along(i, q, z).start()
        lines(go)
        rb[i, z] = pair_sum(i, z)

    def dch(j):
        return pl.ds(pl.multiple_of(j * dc, dc), dc)

    def part_share(i):
        def step(j):
            d, local = dch(j + (i % 2) * npc), dch(j)
            if i < 2:
                term = mm(hs[0], w[2, :, d], 1, 0)
            else:
                term = mm(hs[1], w[0, :, d], 1, 0) + mm(hs[2], w[1, :, d], 1, 0)
            ob[i, :, local] = term.astype(BF16)
        loop(npc, step)
        first_hop(i)

    part_share(0)
    part_share(1)

    peers(lambda p: rank_copy(p, c).wait_recv())
    summed = jnp.zeros(rrb.shape[1:], F32)
    summed = lax.fori_loop(0, n, lambda q, acc: acc + rrb[q].astype(F32), summed)
    rg[:, mine] = (sel[mine, :][None] * summed).astype(BF16)

    def rg_copy(owner, p):
        part = rg.at[:, rows_of(owner)]
        return pltpu.make_async_remote_copy(part, part, rg_send.at[p], rg_recv.at[owner], device_id={"col": p}, device_id_type=MESH)

    peers(lambda p: rg_copy(c, p).start())

    part_share(2)
    second_hop(0)
    part_share(3)
    second_hop(1)

    def local_grads(j):
        f = fch(j)
        guo_ref[:, f] = mm(ur[0], hs[2, :, f], 0, 0).astype(BF16)
        gdi_ref[f, :] = mm(hs[0, :, f], ur[1], 0, 0).astype(BF16)

    loop(nfc, local_grads)
    second_hop(2)
    peers(lambda p: rg_copy(p, c).wait_recv())

    def rank_grads(j):
        d = dch(j)
        gui_ref[d, :] = mm(xg[0, :, d], rg[1], 0, 0).astype(BF16)
        gdo_ref[:, d] = mm(rg[0], xg[1, :, d], 0, 0).astype(BF16)

    loop(ndc, rank_grads)
    second_hop(3)

    def final(i, dest, adapter, contract):
        lines(lambda q: along(i, z, q).wait_recv())
        for j in range(npc):
            d, local = pl.ds((j + (i % 2) * npc) * dc, dc), pl.ds(j * dc, dc)
            total = jnp.zeros((own, dc), F32)
            total = lax.fori_loop(0, half, lambda q, acc, local=local: acc + rb[i, q, :, local].astype(F32), total)
            side = adapter[:, d] if contract == 0 else adapter[d, :]
            dest[:, d] = (total + mm(rg[i // 2, mine], side, 1, contract)).astype(BF16)

    for i in range(4):
        final(i, (out_ref, tg_ref)[i // 2], (do, ui)[i // 2], i // 2)

    rank_x.wait_send()
    for k in range(3):
        loop(nfc, lambda j, k=k: pre_x(k, j).wait_send())
    for i in range(2):
        ag(i, c, partner, partner).wait_send()

    def drain_lines(q):
        for i in range(2):
            ag(i, c, 2 * q + y, 2 * q + y).wait_send()
            ag(i, 2 * q + y, partner, 2 * q + other).wait_send()
        for i in range(4):
            to_partner(i, q).wait_send()
            along(i, q, z).wait_send()
    lines(drain_lines)
    for i in range(4):
        to_partner(i, z).wait_send()

    def drain(p):
        rank_copy(c, p).wait_send()
        rg_copy(c, p).wait_send()
    peers(drain)


def store(*refs):
    count = len(refs) // 2
    sems = refs[-1]
    copies = [pltpu.make_async_copy(refs[i], refs[count + i], sems.at[i]) for i in range(count)]
    for copy in copies:
        copy.start()
    for copy in copies:
        copy.wait()


def per_device(n, tokens, cotangent, adapter_index, retain_mask, gate_weight, up_weight, down_weight, ui, uo, di, do):
    own, width = tokens.shape
    units = gate_weight.shape[0]
    ranks = ui.shape[1]
    group = own * n
    nfc = units // 256 if units % 256 == 0 else 1
    vmem = pl.BlockSpec(memory_space=pltpu.VMEM)
    hbm = pl.BlockSpec(memory_space=pl.ANY)
    dma = pltpu.SemaphoreType.DMA
    V = pltpu.VMEM
    shapes = tuple(
        jax.ShapeDtypeStruct(s, BF16)
        for s in ((own, width), (own, width), (width, ranks), (ranks, units), (units, ranks), (ranks, width))
    )
    held = pl.pallas_call(
        functools.partial(kernel, n),
        out_shape=tuple(V(s.shape, BF16) for s in shapes),
        in_specs=[vmem] * 4 + [hbm] * 7,
        out_specs=tuple([vmem] * 6),
        scratch_shapes=[
            V((3, units, width), BF16), V((width, ranks), BF16), V((ranks, units), BF16), V((units, ranks), BF16), V((ranks, width), BF16),
            V((3, units // BLOCK, width), F32), V((group, ranks), F32), V((2, group, width), BF16),
            V((3, group, units), BF16), V((3, group, units), BF16), V((2, group, ranks), BF16), V((2, group, ranks), BF16),
            V((2, group, ranks), BF16), V((2, group, ranks), F32), V((3, group, units), BF16),
            V((2, group, ranks), BF16), V((n, 2, own, ranks), BF16), V((2, group, ranks), BF16),
            V((4, group, width // 2), BF16), V((4, n // 2, own, width // 2), BF16), V((4, n // 2, own, width // 2), BF16), V((4, n // 2, own, width // 2), BF16),
            dma((3, nfc)), dma((4,)), dma((2, n)), dma((2, n)), dma((3 * nfc + 1,)), dma((3 * nfc + 1,)), dma((n,)), dma((n,)), dma((n,)), dma((n,)),
            dma((4, n // 2)), dma((4, n // 2)), dma((4, n // 2)), dma((4, n // 2)),
        ],
        compiler_params=pltpu.CompilerParams(collective_id=0, has_side_effects=True, vmem_limit_bytes=50 * 1024 * 1024),
    )(tokens, cotangent, adapter_index.reshape(1, group), retain_mask, gate_weight, up_weight, down_weight, ui, uo, di, do)
    return pl.pallas_call(
        store,
        out_shape=shapes,
        in_specs=[vmem] * 6,
        out_specs=tuple([hbm] * 6),
        scratch_shapes=[dma((6,))],
        compiler_params=pltpu.CompilerParams(vmem_limit_bytes=8 * 1024 * 1024),
    )(*(pltpu.with_memory_space_constraint(x, pltpu.VMEM) for x in held))


def solution(mesh):
    return jax.shard_map(
        functools.partial(per_device, mesh.shape["col"]),
        mesh=mesh,
        in_specs=(
            P(("grp", "col"), "row"),
            P(("grp", "col"), "row"),
            P("grp"),
            P(None, "col", "row"),
            P("col", "row"),
            P("col", "row"),
            P("col", "row"),
            P("row", None),
            P(None, "col"),
            P("col", None),
            P(None, "row"),
        ),
        out_specs=(
            P(("grp", "col"), "row"),
            P(("grp", "col"), "row"),
            P(("grp", "row"), None),
            P("grp", "col"),
            P(("grp", "col"), None),
            P("grp", "row"),
        ),
        check_vma=False,
    )
```
